32 devices in a mesh: lat: 4 (over z), ord: 2 (over core), orb: 4 (over y, x).
Axes of the slice: x: 2, y: 2, z: 4, core: 2. Of those that a mesh axis runs over, the one named last changes fastest.
Arguments:
- anomaly: bfloat16 [2, 64, 4320], P(None, 'lat'), may hold values from -6 to 6
- row_weight: float32 [2, 64], replicated, may hold values from 0.2 to 1
- panel: bfloat16 [4, 4, 64, 2, 640], P('orb', None, 'lat', 'ord'), may hold values from -0.5 to 0.5
- order_value: int32 [4, 4], P('orb'), may hold values from 0 to 2159
- deg_first: int32 [4, 4], P('orb', 'lat'), may hold values from 0 to 2190
- sat_rows: bfloat16 [8192, 256], P(('lat', 'ord', 'orb')), may hold values from -0.25 to 0.25
- sat_slot: int32 [8192, 1], P(('lat', 'ord', 'orb')), may hold values from 0 to 15; in each aligned block of 256 rows (0 to 255, 256 to 511, ...) at most 32 rows name the same one
Outputs:
- normals: float32 [4, 4, 2, 640, 2, 640], P('orb', 'lat', 'ord')
- right_side: float32 [4, 4, 2, 2, 640], P('orb', 'lat', None, 'ord')
The draws below stay inside these ranges and needn't reach their ends.
Inputs may be any that keep to these rules, and one draw needn't show every extreme that they name: `sat_slot`: among the 256 rows of one device no order slot appears more than 32 times.
All inputs are finite; a program needn't handle non-finite values.
Results may differ from the reference program's by a relative error of at most 0.0029.
Values may be sent and summed in bfloat16 or wider, within the bound.
A program may use at most 64 MiB of HBM per device.

```python
import math
import jax
import jax.numpy as jnp
import numpy as np
from jax import lax

NLON = 4320
LMAX = 2190
K = 1280
KS = 256
SAT_DEV = 256
NROWS = 64
GROUPS = 4
GORD = 4
ORDERS = 16
CAP = 32
SAT = 8192
N_LAT = 4
N_ORD = 2
N_ORB = 4


def with_ends(result, stream_key, least, high):
    longest = result.shape.index(max(result.shape))
    spots = []
    for shift in (0, 1):
        where = [jax.random.randint(jax.random.fold_in(stream_key, axis), (), 0, length) for axis, length in enumerate(result.shape)]
        where[longest] = (where[longest] + shift) % result.shape[longest]
        spots.append(tuple(where))
    return result.at[spots[0]].set(least).at[spots[1]].set(high)


def steps_of(own_key, extent, split, least, high):
    level, own = 1.0, jax.random.fold_in(own_key, 6)
    for dim, shards_of in split:
        heights = jnp.exp(jax.random.uniform(jax.random.fold_in(own, dim), (shards_of,), jnp.float32, least / len(split), high / len(split)))
        level = level * jnp.repeat(heights, extent[dim] // shards_of).reshape([-1 if axis == dim else 1 for axis in range(len(extent))])
    return level


def routed_block(stream_key, own, number, rows, count, top, bound, skew):
    sequence = jax.random.permutation(stream_key, count)
    crowded, ordinary = shares(count, rows * top, bound, skew, True), shares(count, rows * top, bound, skew, False)
    places = jnp.arange(count)

    def named(lengths, rotation):
        used = int((lengths > 0).sum())
        fixed = max(1, used // 4)
        moved = fixed + (places - fixed + rotation * (used - fixed)) % max(1, count - fixed)
        return jnp.zeros((count,), jnp.int32).at[sequence[jnp.where(places < fixed, places, moved)]].set(jnp.asarray(lengths, jnp.int32))

    lengths = jnp.where(number % 4 == 0, named(crowded, number // 4), named(ordinary, number - number // 4 - 1))
    mixed = jax.random.permutation(jax.random.fold_in(own, 3), count)
    donor, taker = mixed[0:count // 2 * 2:2], mixed[1:count // 2 * 2:2]
    slack = jnp.minimum(lengths[donor] - 1, bound - lengths[taker]) // 2
    slack = jnp.where((donor == sequence[0]) | (taker == sequence[0]) | (lengths[taker] == 0), 0, jnp.maximum(slack, 0))
    moved = jax.random.randint(jax.random.fold_in(own, 4), (count // 2,), 0, 1 << 20) % (slack + 1)
    lengths = lengths.at[donor].add(-moved).at[taker].add(moved)
    items = jnp.searchsorted(jnp.cumsum(lengths), jnp.arange(rows * top), side="right").astype(jnp.int32)
    listing = items.reshape(top, rows).T
    listing = listing[jax.random.permutation(jax.random.fold_in(own, 1), rows)]
    rotation = jax.random.randint(jax.random.fold_in(own, 2), (rows, 1), 0, top)
    return jnp.take_along_axis(listing, (jnp.arange(top)[None, :] + rotation) % top, axis=1)


def shares(number_of, total, most, lean, full):
    weights = [(1 << 20) // math.isqrt(rank ** lean) + 1 for rank in range(1, number_of + 1)]
    largest = most if full else min(most, max(-(-total // number_of), total * weights[0] // sum(weights)))
    least = 1 if total - largest >= number_of - 1 else 0
    holding, rest = [largest] + [least] * (number_of - 1), total - largest - least * (number_of - 1)
    while rest > 0:
        movable = [i for i in range(1, number_of) if holding[i] < largest] or [i for i in range(1, number_of) if holding[i] < most]
        mass, left = sum([weights[i] for i in movable]), rest
        for i in movable:
            extra = min(most - holding[i], max(1, left * weights[i] // mass), rest)
            holding[i] = holding[i] + extra
            rest = rest - extra
    return np.array(holding)


def centred(stream_key, dims, deviation, most, split=(), kind=jnp.bfloat16):
    gain = steps_of(stream_key, dims, split, -0.22, 0.18) if split else 1.0
    array = jax.random.normal(stream_key, dims, jnp.float32) * deviation * gain
    return jnp.minimum(jnp.maximum(array, -most), most).astype(kind)


def setup_inputs(seed: int = 0) -> dict:
    key_list = jax.random.split(jax.random.key(seed), 8)
    anomaly = centred(key_list[0], (2, NROWS, NLON), 1.0, 6.0, ((1, 4),))
    row_weight = jnp.clip(jnp.exp(jax.random.uniform(key_list[1], (2, NROWS), jnp.float32, math.log(0.2), math.log(1.0))), 0.2, 1.0)
    panel = centred(key_list[2], (GROUPS, GORD, NROWS, 2, K // 2), (2 * NROWS) ** -0.5, 0.5, ((0, 4), (2, 4), (3, 2)))
    order_value = with_ends(jax.random.randint(key_list[3], (GROUPS, GORD), 0, NLON // 2), jax.random.fold_in(key_list[3], 1), 0, (NLON // 2) - 1).astype(jnp.int32)
    deg_first = with_ends(jax.random.randint(key_list[4], (GROUPS, GORD), 0, LMAX + 1), jax.random.fold_in(key_list[4], 1), 0, LMAX).astype(jnp.int32)
    sat_rows = centred(key_list[5], (SAT, KS), (SAT_DEV * N_LAT * N_ORD * N_ORB // ORDERS) ** -0.5, 0.25, ((0, 32),))
    sat_slot_keys = jax.random.split(jax.random.fold_in(key_list[6], 1), SAT // SAT_DEV)
    sat_slot_turns = jax.random.permutation(jax.random.fold_in(key_list[6], 3), SAT // SAT_DEV)
    sat_slot = jax.vmap(lambda own, number: routed_block(jax.random.fold_in(key_list[6], 2), own, number, SAT_DEV, ORDERS, 1, CAP, 2))(sat_slot_keys, sat_slot_turns).reshape((SAT, 1))
    return {"anomaly": anomaly, "row_weight": row_weight, "panel": panel, "order_value": order_value, "deg_first": deg_first, "sat_rows": sat_rows, "sat_slot": sat_slot}


def reference(anomaly, row_weight, panel, order_value, deg_first, sat_rows, sat_slot):
    half_count = K // 2
    half_sat = KS // 2
    order_flat = order_value.reshape(-1).astype(jnp.int32)
    first_flat = deg_first.reshape(-1).astype(jnp.int32)
    parity_col = jnp.arange(2, dtype=jnp.int32)[:, None] + 2 * jnp.arange(half_count, dtype=jnp.int32)[None, :]
    degree = first_flat[:, None, None] + parity_col[None]
    live_flags = (degree <= LMAX).astype(jnp.float32)
    parity_sign = 1.0 - 2.0 * ((degree + order_flat[:, None, None]) % 2).astype(jnp.float32)
    spectra = jnp.fft.rfft(anomaly.astype(jnp.float32), axis=-1)[:, :, order_flat]
    scale_factor = math.sqrt(2.0 / NLON)
    cos_part = (jnp.real(spectra) * scale_factor).astype(jnp.float32)
    sin_part = (-jnp.imag(spectra) * scale_factor).astype(jnp.float32)
    weight_north = row_weight[0][:, None]
    weight_south = row_weight[1][:, None]
    coefficients = jnp.stack([weight_north * cos_part[0], weight_north * sin_part[0], weight_south * cos_part[1], weight_south * sin_part[1]], axis=-1).astype(jnp.bfloat16)
    coefficients = jnp.transpose(coefficients, (1, 0, 2))
    panel_flat = panel.reshape(-1, NROWS, 2, half_count)
    plus_weight = (row_weight[0] + row_weight[1])[:, None, None]
    minus_weight = (row_weight[0] - row_weight[1])[:, None, None]
    device_total = N_LAT * N_ORD * N_ORB
    order_total = order_flat.shape[0]
    sat_by_device = sat_rows.reshape(device_total, SAT_DEV, KS)
    slot_by_device = sat_slot.reshape(device_total, SAT_DEV).astype(jnp.int32)
    position = jnp.arange(SAT_DEV, dtype=jnp.int32)

    def add_device(total, pieces):
        rows_one, slot_one = pieces
        earlier = (slot_one[:, None] == slot_one[None, :]) & (position[None, :] < position[:, None])
        slot_rank = lax.optimization_barrier(jnp.sum(earlier, axis=1, dtype=jnp.int32))
        target = slot_one * CAP + slot_rank
        bucket = jnp.zeros((order_total * CAP, KS), jnp.float32).at[target].set(rows_one.astype(jnp.float32))
        bucket = bucket.reshape(order_total, CAP, KS)
        return (total + jnp.einsum('ock,ocl->okl', bucket, bucket, precision=lax.Precision.HIGHEST), None)
    sat_normal, _ = lax.scan(add_device, jnp.zeros((order_total, KS, KS), jnp.float32), (sat_by_device, slot_by_device))
    sat_parity = sat_normal.reshape(order_total, half_sat, 2, half_sat, 2).transpose(0, 2, 1, 4, 3)

    def per_order(pieces):
        panel_one, live_one, sign_one, coef_one, sat_one = pieces
        masked = (panel_one.astype(jnp.float32) * live_one[None]).astype(jnp.bfloat16)
        plus_panel = (masked.astype(jnp.float32) * plus_weight).astype(jnp.bfloat16)
        minus_panel = (masked.astype(jnp.float32) * minus_weight).astype(jnp.bfloat16)
        masked_wide = masked.astype(jnp.float32)
        plus_wide = plus_panel.astype(jnp.float32)
        minus_wide = minus_panel.astype(jnp.float32)
        same_block = jnp.einsum('rpi,rpj->pij', masked_wide, plus_wide, precision=lax.Precision.HIGHEST)
        cross_block = jnp.einsum('rpi,rpj->pij', masked_wide, minus_wide[:, ::-1], precision=lax.Precision.HIGHEST)
        upper_rows = jnp.stack([same_block[0], cross_block[0]], axis=1)
        lower_rows = jnp.stack([cross_block[1], same_block[1]], axis=1)
        grid_normal = jnp.stack([upper_rows, lower_rows], axis=0)
        sat_full = jnp.pad(sat_one, ((0, 0), (0, half_count - half_sat), (0, 0), (0, half_count - half_sat)))
        normal_one = grid_normal + sat_full * (live_one[:, :, None, None] * live_one[None, None, :, :])
        products = jnp.einsum('rpi,rc->cpi', masked_wide, coef_one.astype(jnp.float32), precision=lax.Precision.HIGHEST)
        right_one = jnp.stack([products[0] + sign_one * products[2], products[1] + sign_one * products[3]])
        return (normal_one, right_one)
    normal_all, right_all = lax.map(per_order, (panel_flat, live_flags, parity_sign, coefficients, sat_parity))
    return (normal_all.reshape(GROUPS, GORD, 2, half_count, 2, half_count), right_all.reshape(GROUPS, GORD, 2, 2, half_count))
```

```python
import functools
import math

import jax
import jax.numpy as jnp
from jax import lax
from jax.experimental import pallas as pl
from jax.experimental.pallas import tpu as pltpu
from jax.experimental.layout import Layout, with_layout_constraint
from jax.sharding import PartitionSpec as P

LMAX = 2190
MESH = pl.DeviceIdType.MESH
F32 = jnp.float32
BF16 = jnp.bfloat16
LANES = 128


def iota(shape, dim):
    return lax.broadcasted_iota(jnp.int32, shape, dim)


def dot_tn(a, b):
    return lax.dot_general(a, b, (((0,), (0,)), ((), ())), preferred_element_type=F32)


def dot_nt(a, b):
    return lax.dot_general(a, b, (((1,), (1,)), ((), ())), preferred_element_type=F32)


def dot_nn(a, b):
    return jnp.dot(a, b, preferred_element_type=F32)


def exchange_kernel(
    sizes,
    anomaly, weight, panel, order, sat_rows, slot_row,
    panels, coefs, sat_out,
    bucket, arrived, coef_mine, gram_send, gram_recv,
    panel_s, panel_r, coef_s, coef_r, sat_s, sat_r, pair_s, pair_r,
):
    n_lat, n_orb = sizes
    group_orders, row_count, half_count = panel.shape
    sat_count, width = sat_rows.shape
    half = width // 2
    cap = bucket.shape[1]
    slots = bucket.shape[0]
    n_src = n_lat * n_orb
    lon = anomaly.shape[2]
    lat = lax.axis_index("lat")
    par = lax.axis_index("ord")
    orb = lax.axis_index("orb")
    other = 1 - par
    me = lat * n_orb + orb

    def peer(k):
        p = lax.rem(me + k, n_src)
        return p, p // n_orb, lax.rem(p, n_orb)

    barrier = pltpu.get_barrier_semaphore()
    pl.semaphore_signal(barrier, inc=1, device_id=(lat, other, orb), device_id_type=MESH)

    def greet(k, c):
        _, a, b = peer(k)
        pl.semaphore_signal(barrier, inc=1, device_id=(a, par, b), device_id_type=MESH)
        return c

    lax.fori_loop(1, n_src, greet, 0)

    perm = (iota((width, width), 0)
            == 2 * (iota((width, width), 1) % half) + iota((width, width), 1) // half)
    split_rows = dot_nn(sat_rows[...], perm.astype(F32).astype(BF16)).astype(BF16)
    row = slot_row[...].astype(F32)
    sub = iota((sat_count, sat_count), 0)
    lane = iota((sat_count, sat_count), 1)
    column = jnp.sum(jnp.where(sub == lane, row, 0.0), axis=1, keepdims=True)
    earlier = (column == row) & (sub < lane)
    rank = jnp.sum(jnp.where(earlier, 1.0, 0.0), axis=0, keepdims=True)
    target = row * float(cap) + rank
    step_slots = max(1, min(slots, 512 // cap))

    def fill(i, c):
        spot = (iota((step_slots * cap, sat_count), 0) + i * (step_slots * cap)).astype(F32)
        hot = jnp.where(spot == target, 1.0, 0.0).astype(BF16)
        rows = dot_nn(hot, split_rows).astype(BF16)
        bucket[pl.ds(i * step_slots, step_slots)] = rows.reshape(step_slots, cap, width)
        return c

    if slots == step_slots:
        fill(0, 0)
    else:
        lax.fori_loop(0, slots // step_slots, fill, 0)

    pl.semaphore_wait(barrier, n_src)

    def panel_copy(dst, src):
        return pltpu.make_async_remote_copy(
            src_ref=panel.at[dst], dst_ref=panels.at[par, src],
            send_sem=panel_s.at[dst], recv_sem=panel_r.at[src],
            device_id=(dst, par, orb), device_id_type=MESH)

    def sat_copy(dst, a, b, src):
        return pltpu.make_async_remote_copy(
            src_ref=bucket.at[b * group_orders + a], dst_ref=arrived.at[src],
            send_sem=sat_s.at[dst], recv_sem=sat_r.at[src],
            device_id=(a, par, b), device_id_type=MESH)

    def coef_copy(dst, src):
        return pltpu.make_async_remote_copy(
            src_ref=coef_mine, dst_ref=coefs.at[src],
            send_sem=coef_s.at[dst], recv_sem=coef_r.at[src],
            device_id=(dst, par, orb), device_id_type=MESH)

    def forward():
        return pltpu.make_async_remote_copy(
            src_ref=panels.at[par], dst_ref=panels.at[par],
            send_sem=pair_s.at[0], recv_sem=pair_r.at[0],
            device_id=(lat, other, orb), device_id_type=MESH)

    def backward():
        return pltpu.make_async_remote_copy(
            src_ref=panels.at[par], dst_ref=panels.at[other],
            send_sem=pair_s.at[0], recv_sem=pair_r.at[0],
            device_id=(lat, other, orb), device_id_type=MESH)

    def gram_copy():
        return pltpu.make_async_remote_copy(
            src_ref=gram_send, dst_ref=gram_recv,
            send_sem=pair_s.at[1], recv_sem=pair_r.at[1],
            device_id=(lat, other, orb), device_id_type=MESH)

    def each_lat(action):
        def body(k, c):
            action(lax.rem(lat + k, n_lat))
            return c

        lax.fori_loop(1, n_lat, body, 0)

    def each_src(action):
        def body(k, c):
            action(*peer(k))
            return c

        lax.fori_loop(1, n_src, body, 0)

    each_lat(lambda dst: panel_copy(dst, lat).start())
    each_src(lambda p, a, b: sat_copy(p, a, b, me).start())
    arrived[me] = bucket[orb * group_orders + lat]
    panels[par, lat] = panel[lat]

    wide = 2 * group_orders
    line = iota((wide, group_orders), 0)
    pick = lax.rem(line, group_orders) == iota((wide, group_orders), 1)
    order_col = jnp.sum(
        jnp.where(pick, order[...].astype(F32), 0.0), axis=1, keepdims=True)
    sample = iota((wide, lon), 1).astype(F32)
    x = sample * order_col
    r = x - jnp.floor(x * (1.0 / lon)) * float(lon)
    r = r - jnp.where(iota((wide, lon), 0) >= group_orders, lon / 4.0, 0.0)
    r = r - jnp.floor(r * (1.0 / lon) + 0.5) * float(lon)
    z = (lon / 4.0 - jnp.abs(r)) * (2.0 * math.pi / lon)
    z2 = z * z
    poly = -1.0 / math.factorial(11)
    for d in (9, 7, 5, 3, 1):
        sgn = 1.0 if d % 4 == 1 else -1.0
        poly = poly * z2 + sgn / math.factorial(d)
    trig = poly * z
    high = trig.astype(BF16)
    low = (trig - high.astype(F32)).astype(BF16)
    coef_mine[...] = jnp.zeros_like(coef_mine)
    total_rows = weight.shape[1]
    here = (iota((row_count, total_rows), 1)
            == iota((row_count, total_rows), 0) + lat * row_count)
    scale = math.sqrt(2.0 / lon)
    for h in range(2):
        data = anomaly[h]
        spectrum = (dot_nt(data, high) + dot_nt(data, low)) * scale
        own_weight = jnp.sum(
            jnp.where(here, weight[h:h + 1, :], 0.0), axis=1, keepdims=True)
        coef_mine[h, :, 0:wide] = (spectrum * own_weight).astype(BF16)
    each_lat(lambda dst: coef_copy(dst, lat).start())
    coefs[lat] = coef_mine[...]

    each_lat(lambda src: panel_copy(src, src).wait_recv())
    forward().start()
    each_src(lambda p, a, b: sat_copy(p, a, b, p).wait_recv())

    chunk = max(1, min(n_src, 512 // cap))
    steps = n_src // chunk

    def gram(which):
        cols = pl.ds(pl.multiple_of(which * half, half), half)

        def part(i):
            full = arrived[pl.ds(i * chunk, chunk)].reshape(chunk * cap, width)
            some = arrived[pl.ds(i * chunk, chunk), :, cols].reshape(chunk * cap, half)
            return dot_tn(some, full)

        if steps == 1:
            return part(0)
        return lax.fori_loop(
            0, steps, lambda i, c: c + part(i), jnp.zeros((half, width), F32))

    gram_send[...] = gram(other)
    gram_copy().start()
    own = gram(par)
    each_lat(lambda src: coef_copy(src, src).wait_recv())
    backward().wait_recv()
    gram_copy().wait_recv()
    sat_out[...] = own + gram_recv[...]
    each_lat(lambda dst: panel_copy(dst, lat).wait_send())
    each_lat(lambda dst: coef_copy(dst, lat).wait_send())
    each_src(lambda p, a, b: sat_copy(p, a, b, me).wait_send())
    forward().wait_send()
    gram_copy().wait_send()


def normal_kernel(order, first, weight, panels, coefs, sat, out, right, left, sides):
    step = pl.program_id(0)
    lat = lax.axis_index("lat")
    par = lax.axis_index("ord")
    _, n_lat, row_count, half_count = panels.shape
    total = n_lat * row_count
    tile, width = sat.shape
    stripes = half_count // LANES
    base = first[0, 0]
    group_orders = order.shape[1]
    limit = LMAX - base

    @pl.when(step == 0)
    def _():
        for l in range(n_lat):
            rows = slice(l * row_count, (l + 1) * row_count)
            here = (iota((row_count, total), 1) == iota((row_count, total), 0) + l * row_count)
            north = jnp.sum(jnp.where(here, weight[0:1, :], 0.0), axis=1, keepdims=True)
            south = jnp.sum(jnp.where(here, weight[1:2, :], 0.0), axis=1, keepdims=True)
            for q in range(2):
                live = 2 * iota((row_count, half_count), 1) + q <= limit
                masked = jnp.where(live, panels[q, l].astype(F32), 0.0)
                factor = jnp.where(par == q, north + south, north - south)
                sides[q, rows, :] = (masked * factor).astype(BF16)
            live = 2 * iota((row_count, half_count), 1) + par <= limit
            left[rows, :] = jnp.where(live, panels[par, l].astype(F32), 0.0).astype(BF16)
        sign = 1.0 - 2.0 * lax.rem(base + par + order[0, lat], 2).astype(F32)
        masked = left[...]
        north = dot_tn(coefs[:, 0].reshape(total, LANES), masked)
        south = dot_tn(coefs[:, 1].reshape(total, LANES), masked)
        both = north + sign * south
        place = iota((LANES, half_count), 0)
        for t in range(2):
            right[t] = jnp.sum(
                jnp.where(place == t * group_orders + lat, both, 0.0), axis=0, keepdims=True)

    cols = pl.ds(pl.multiple_of(step * tile, tile), tile)
    block = left[:, cols]
    for q in range(2):
        value = dot_tn(block, sides[q])
        for b in range(stripes):
            out[pl.ds(2 * b + q, tile, stride=2 * stripes), :] = (
                value[:, b * LANES:(b + 1) * LANES])

    @pl.when(step == 0)
    def _():
        half = width // 2
        for q in range(2):
            for b in range(half // LANES):
                at = pl.ds(2 * b + q, tile, stride=2 * stripes)
                keep = ((2 * iota((tile, LANES), 0) + par <= limit)
                        & (2 * (iota((tile, LANES), 1) + b * LANES) + q <= limit))
                piece = sat[:, q * half + b * LANES:q * half + (b + 1) * LANES]
                out[at, :] = out[at, :] + jnp.where(keep, piece, 0.0)


def shards(sizes, anomaly, row_weight, panel, order_value, deg_first, sat_rows, sat_slot):
    n_lat, n_orb = sizes
    _, group_orders, row_count, _, half_count = panel.shape
    sat_count, width = sat_rows.shape
    half = width // 2
    total = n_lat * row_count
    slots = n_orb * group_orders
    n_src = n_lat * n_orb
    cap = max(16, 2 * sat_count // slots)
    vmem = pl.BlockSpec(memory_space=pltpu.VMEM)
    smem = pl.BlockSpec(memory_space=pltpu.SMEM)
    dma = pltpu.SemaphoreType.DMA
    panels, coefs, sat = pl.pallas_call(
        functools.partial(exchange_kernel, sizes),
        out_shape=(
            jax.ShapeDtypeStruct((2, n_lat, row_count, half_count), BF16),
            jax.ShapeDtypeStruct((n_lat, 2, row_count, LANES), BF16),
            jax.ShapeDtypeStruct((half, width), F32),
        ),
        in_specs=[vmem] * 6,
        out_specs=[vmem] * 3,
        scratch_shapes=[
            pltpu.VMEM((slots, cap, width), BF16),
            pltpu.VMEM((n_src, cap, width), BF16),
            pltpu.VMEM((2, row_count, LANES), BF16),
            pltpu.VMEM((half, width), F32),
            pltpu.VMEM((half, width), F32),
            dma((n_lat,)), dma((n_lat,)), dma((n_lat,)), dma((n_lat,)),
            dma((n_src,)), dma((n_src,)), dma((2,)), dma((2,)),
        ],
        compiler_params=pltpu.CompilerParams(
            collective_id=0, has_side_effects=True, vmem_limit_bytes=40 * 2**20),
        name="exchange",
    )(
        anomaly,
        row_weight,
        panel.reshape(group_orders, row_count, half_count),
        order_value,
        sat_rows,
        sat_slot.reshape(1, sat_count),
    )
    stripes = half_count // LANES
    flat, right = pl.pallas_call(
        normal_kernel,
        grid=(half_count // half,),
        out_shape=(
            jax.ShapeDtypeStruct((half_count * 2 * stripes, LANES), F32),
            jax.ShapeDtypeStruct((2, 1, half_count), F32),
        ),
        in_specs=[smem, smem, vmem, vmem, vmem, vmem],
        out_specs=[
            pl.BlockSpec((half * 2 * stripes, LANES), lambda i: (i, 0)),
            pl.BlockSpec((2, 1, half_count), lambda i: (0, 0, 0)),
        ],
        scratch_shapes=[
            pltpu.VMEM((total, half_count), BF16),
            pltpu.VMEM((2, total, half_count), BF16),
        ],
        compiler_params=pltpu.CompilerParams(
            dimension_semantics=("arbitrary",), vmem_limit_bytes=40 * 2**20),
        name="normal",
    )(order_value, deg_first, row_weight, panels, coefs, sat)
    normals = flat.reshape(half_count, stripes, 2, LANES).transpose(0, 2, 1, 3)
    normals = with_layout_constraint(normals, Layout((0, 2, 1, 3)))
    normals = normals.reshape(1, 1, 1, half_count, 2, half_count)
    return normals, right.reshape(1, 1, 2, 1, half_count)


def solution(mesh):
    sizes = (mesh.shape["lat"], mesh.shape["orb"])
    in_specs = (
        P(None, "lat", None),
        P(),
        P("orb", None, "lat", "ord", None),
        P("orb", None),
        P("orb", "lat"),
        P(("lat", "ord", "orb"), None),
        P(("lat", "ord", "orb"), None),
    )
    out_specs = (P("orb", "lat", "ord", None, None, None), P("orb", "lat", None, "ord", None))
    return jax.shard_map(
        functools.partial(shards, sizes), mesh=mesh, in_specs=in_specs,
        out_specs=out_specs, check_vma=False)
```

```python
import functools
import math

import jax
import jax.numpy as jnp
from jax import lax
from jax.experimental import pallas as pl
from jax.experimental.pallas import tpu as pltpu
from jax.experimental.layout import Layout, with_layout_constraint
from jax.sharding import PartitionSpec as P

LMAX = 2190
MESH = pl.DeviceIdType.MESH
F32 = jnp.float32
BF16 = jnp.bfloat16
LANES = 128


def iota(shape, dim):
    return lax.broadcasted_iota(jnp.int32, shape, dim)


def dot_tn(a, b):
    return lax.dot_general(a, b, (((0,), (0,)), ((), ())), preferred_element_type=F32)


def dot_nt(a, b):
    return lax.dot_general(a, b, (((1,), (1,)), ((), ())), preferred_element_type=F32)


def dot_nn(a, b):
    return jnp.dot(a, b, preferred_element_type=F32)


def exchange_kernel(
    sizes,
    order, first, anomaly_hbm, weight_hbm, panel, sat_hbm, slot_hbm,
    out_hbm, right_hbm,
    out, right, anomaly, weight, sat_rows, slot_row, panels, coefs,
    bucket, arrived, coef_mine, gram_send, gram_recv, left, sides,
    load, save, panel_s, panel_r, coef_s, coef_r, sat_s, sat_r, pair_s, pair_r,
):
    n_lat, n_orb = sizes
    group_orders, row_count, half_count = panel.shape
    sat_count, width = sat_rows.shape
    half = width // 2
    cap = bucket.shape[1]
    slots = bucket.shape[0]
    n_src = n_lat * n_orb
    lon = anomaly.shape[2]
    lat = lax.axis_index("lat")
    par = lax.axis_index("ord")
    orb = lax.axis_index("orb")
    other = 1 - par
    stripes = half_count // LANES
    base = first[0, 0]
    limit = LMAX - base
    me = lat * n_orb + orb

    def peer(k):
        p = lax.rem(me + k, n_src)
        return p, p // n_orb, lax.rem(p, n_orb)

    loads = [
        pltpu.make_async_copy(sat_hbm, sat_rows, load.at[0]),
        pltpu.make_async_copy(slot_hbm, slot_row, load.at[1]),
        pltpu.make_async_copy(anomaly_hbm, anomaly, load.at[2]),
        pltpu.make_async_copy(weight_hbm, weight, load.at[3]),
        pltpu.make_async_copy(panel.at[lat], panels.at[par, lat], load.at[4]),
    ]
    for one in loads:
        one.start()
    barrier = pltpu.get_barrier_semaphore()
    pl.semaphore_signal(barrier, inc=1, device_id=(lat, other, orb), device_id_type=MESH)

    def greet(k, c):
        _, a, b = peer(k)
        pl.semaphore_signal(barrier, inc=1, device_id=(a, par, b), device_id_type=MESH)
        return c

    lax.fori_loop(1, n_src, greet, 0)

    def panel_copy(dst, src):
        return pltpu.make_async_remote_copy(
            src_ref=panel.at[dst], dst_ref=panels.at[par, src],
            send_sem=panel_s.at[dst], recv_sem=panel_r.at[src],
            device_id=(dst, par, orb), device_id_type=MESH)

    def sat_copy(dst, a, b, src):
        return pltpu.make_async_remote_copy(
            src_ref=bucket.at[b * group_orders + a], dst_ref=arrived.at[src],
            send_sem=sat_s.at[dst], recv_sem=sat_r.at[src],
            device_id=(a, par, b), device_id_type=MESH)

    def coef_copy(dst, src):
        return pltpu.make_async_remote_copy(
            src_ref=coef_mine, dst_ref=coefs.at[src],
            send_sem=coef_s.at[dst], recv_sem=coef_r.at[src],
            device_id=(dst, par, orb), device_id_type=MESH)

    def forward():
        return pltpu.make_async_remote_copy(
            src_ref=panels.at[par], dst_ref=panels.at[par],
            send_sem=pair_s.at[0], recv_sem=pair_r.at[0],
            device_id=(lat, other, orb), device_id_type=MESH)

    def backward():
        return pltpu.make_async_remote_copy(
            src_ref=panels.at[par], dst_ref=panels.at[other],
            send_sem=pair_s.at[0], recv_sem=pair_r.at[0],
            device_id=(lat, other, orb), device_id_type=MESH)

    def gram_copy():
        return pltpu.make_async_remote_copy(
            src_ref=gram_send, dst_ref=gram_recv,
            send_sem=pair_s.at[1], recv_sem=pair_r.at[1],
            device_id=(lat, other, orb), device_id_type=MESH)

    def each_lat(action):
        def body(k, c):
            action(lax.rem(lat + k, n_lat))
            return c

        lax.fori_loop(1, n_lat, body, 0)

    def each_src(action):
        def body(k, c):
            action(*peer(k))
            return c

        lax.fori_loop(1, n_src, body, 0)

    loads[0].wait()
    loads[1].wait()
    perm = (iota((width, width), 0)
            == 2 * (iota((width, width), 1) % half) + iota((width, width), 1) // half)
    split_rows = dot_nn(sat_rows[...], perm.astype(F32).astype(BF16)).astype(BF16)
    row = slot_row[...].astype(F32)
    sub = iota((sat_count, sat_count), 0)
    lane = iota((sat_count, sat_count), 1)
    column = jnp.sum(jnp.where(sub == lane, row, 0.0), axis=1, keepdims=True)
    earlier = (column == row) & (sub < lane)
    rank = jnp.sum(jnp.where(earlier, 1.0, 0.0), axis=0, keepdims=True)
    target = row * float(cap) + rank
    pl.semaphore_wait(barrier, n_src)
    each_lat(lambda dst: panel_copy(dst, lat).start())
    step_slots = max(1, min(slots, 512 // cap))

    def fill(i, c):
        spot = (iota((step_slots * cap, sat_count), 0) + i * (step_slots * cap)).astype(F32)
        hot = jnp.where(spot == target, 1.0, 0.0).astype(BF16)
        rows = dot_nn(hot, split_rows).astype(BF16)
        bucket[pl.ds(i * step_slots, step_slots)] = rows.reshape(step_slots, cap, width)
        return c

    if slots == step_slots:
        fill(0, 0)
    else:
        lax.fori_loop(0, slots // step_slots, fill, 0)

    each_src(lambda p, a, b: sat_copy(p, a, b, me).start())
    arrived[me] = bucket[orb * group_orders + lat]
    loads[2].wait()
    loads[3].wait()
    loads[4].wait()

    wide = 2 * group_orders
    line = iota((wide, 1), 0)
    order_col = jnp.zeros((wide, 1), F32)
    for o in range(group_orders):
        order_col = jnp.where(
            lax.rem(line, group_orders) == o, order[0, o].astype(F32), order_col)
    sample = iota((wide, lon), 1).astype(F32)
    x = sample * order_col
    r = x - jnp.floor(x * (1.0 / lon)) * float(lon)
    r = r - jnp.where(iota((wide, lon), 0) >= group_orders, lon / 4.0, 0.0)
    r = r - jnp.floor(r * (1.0 / lon) + 0.5) * float(lon)
    z = (lon / 4.0 - jnp.abs(r)) * (2.0 * math.pi / lon)
    z2 = z * z
    poly = -1.0 / math.factorial(11)
    for d in (9, 7, 5, 3, 1):
        sgn = 1.0 if d % 4 == 1 else -1.0
        poly = poly * z2 + sgn / math.factorial(d)
    trig = poly * z
    high = trig.astype(BF16)
    low = (trig - high.astype(F32)).astype(BF16)
    coef_mine[...] = jnp.zeros_like(coef_mine)
    total_rows = weight.shape[1]
    here = (iota((row_count, total_rows), 1)
            == iota((row_count, total_rows), 0) + lat * row_count)
    scale = math.sqrt(2.0 / lon)
    for h in range(2):
        data = anomaly[h]
        spectrum = (dot_nt(data, high) + dot_nt(data, low)) * scale
        own_weight = jnp.sum(
            jnp.where(here, weight[h:h + 1, :], 0.0), axis=1, keepdims=True)
        coef_mine[:, h * wide:(h + 1) * wide] = (spectrum * own_weight).astype(BF16)
    each_lat(lambda dst: coef_copy(dst, lat).start())
    coefs[lat] = coef_mine[...]

    each_lat(lambda src: panel_copy(src, src).wait_recv())
    forward().start()
    for l in range(n_lat):
        rows = slice(l * row_count, (l + 1) * row_count)
        live = 2 * iota((row_count, half_count), 1) + par <= limit
        left[rows, :] = jnp.where(live, panels[par, l].astype(F32), 0.0).astype(BF16)
    each_lat(lambda src: coef_copy(src, src).wait_recv())
    sign = 1.0 - 2.0 * lax.rem(base + par + order[0, lat], 2).astype(F32)
    products = dot_tn(coefs[...].reshape(total_rows, coefs.shape[2]), left[...])
    place = iota(products.shape, 0)
    for t in range(2):
        spot = t * group_orders + lat
        factor = jnp.where(place == spot, 1.0, jnp.where(place == wide + spot, sign, 0.0))
        right[t] = jnp.sum(products * factor, axis=0, keepdims=True)
    backward().wait_recv()
    for l in range(n_lat):
        rows = slice(l * row_count, (l + 1) * row_count)
        here = (iota((row_count, total_rows), 1)
                == iota((row_count, total_rows), 0) + l * row_count)
        north = jnp.sum(jnp.where(here, weight[0:1, :], 0.0), axis=1, keepdims=True)
        south = jnp.sum(jnp.where(here, weight[1:2, :], 0.0), axis=1, keepdims=True)
        for q in range(2):
            live = 2 * iota((row_count, half_count), 1) + q <= limit
            masked = jnp.where(live, panels[q, l].astype(F32), 0.0)
            factor = jnp.where(par == q, north + south, north - south)
            sides[q, rows, :] = (masked * factor).astype(BF16)

    def grid_tile(i):
        block = left[:, i * half:(i + 1) * half]
        for q in range(2):
            value = dot_tn(block, sides[q])
            for b in range(stripes):
                at = pl.ds(i * half * 2 * stripes + 2 * b + q, half, stride=2 * stripes)
                out[at, :] = value[:, b * LANES:(b + 1) * LANES]

    def save_tile(i):
        span = pl.ds(i * half * 2 * stripes, half * 2 * stripes)
        return pltpu.make_async_copy(out.at[span], out_hbm.at[span], save.at[i])

    tiles = half_count // half
    save_right = pltpu.make_async_copy(right, right_hbm, save.at[tiles])
    save_right.start()
    for i in range(1, tiles):
        grid_tile(i)
        save_tile(i).start()
    each_src(lambda p, a, b: sat_copy(p, a, b, p).wait_recv())

    chunk = max(1, min(n_src, 512 // cap))
    steps = n_src // chunk

    def gram(which):
        cols = pl.ds(pl.multiple_of(which * half, half), half)

        def part(i):
            full = arrived[pl.ds(i * chunk, chunk)].reshape(chunk * cap, width)
            some = arrived[pl.ds(i * chunk, chunk), :, cols].reshape(chunk * cap, half)
            return dot_tn(some, full)

        if steps == 1:
            return part(0)
        return lax.fori_loop(
            0, steps, lambda i, c: c + part(i), jnp.zeros((half, width), F32))

    gram_send[...] = gram(other)
    gram_copy().start()
    own = gram(par)
    grid_tile(0)
    gram_copy().wait_recv()
    summed = own + gram_recv[...]
    for q in range(2):
        for b in range(half // LANES):
            at = pl.ds(2 * b + q, half, stride=2 * stripes)
            keep = ((2 * iota((half, LANES), 0) + par <= limit)
                    & (2 * (iota((half, LANES), 1) + b * LANES) + q <= limit))
            piece = summed[:, q * half + b * LANES:q * half + (b + 1) * LANES]
            out[at, :] = out[at, :] + jnp.where(keep, piece, 0.0)
    save_tile(0).start()
    each_lat(lambda dst: panel_copy(dst, lat).wait_send())
    each_lat(lambda dst: coef_copy(dst, lat).wait_send())
    each_src(lambda p, a, b: sat_copy(p, a, b, me).wait_send())
    forward().wait_send()
    gram_copy().wait_send()
    save_right.wait()
    for i in range(tiles):
        save_tile(i).wait()


def hand_out(flat, side, out, right, sem):
    parts = sem.shape[0] - 1
    rows = flat.shape[0] // parts
    copies = [pltpu.make_async_copy(side, right, sem.at[parts])]
    for i in range(parts):
        span = pl.ds(i * rows, rows)
        copies.append(pltpu.make_async_copy(flat.at[span], out.at[span], sem.at[i]))
    for one in copies:
        one.start()
    for one in copies:
        one.wait()


def shards(sizes, anomaly, row_weight, panel, order_value, deg_first, sat_rows, sat_slot):
    n_lat, n_orb = sizes
    _, group_orders, row_count, _, half_count = panel.shape
    sat_count, width = sat_rows.shape
    half = width // 2
    total = n_lat * row_count
    slots = n_orb * group_orders
    n_src = n_lat * n_orb
    cap = max(16, 2 * sat_count // slots)
    smem = pl.BlockSpec(memory_space=pltpu.SMEM)
    dma = pltpu.SemaphoreType.DMA
    hbm = pl.BlockSpec(memory_space=pltpu.HBM)
    stripes = half_count // LANES
    coef_width = -(-4 * group_orders // LANES) * LANES
    results = (
        jax.ShapeDtypeStruct((half_count * 2 * stripes, LANES), F32),
        jax.ShapeDtypeStruct((2, 1, half_count), F32),
    )
    flat, right = pl.pallas_call(
        functools.partial(exchange_kernel, sizes),
        out_shape=results,
        in_specs=[smem] * 2 + [hbm] * 5,
        out_specs=[hbm] * 2,
        scratch_shapes=[
            pltpu.VMEM(results[0].shape, F32),
            pltpu.VMEM(results[1].shape, F32),
            pltpu.VMEM(anomaly.shape, BF16),
            pltpu.VMEM(row_weight.shape, F32),
            pltpu.VMEM(sat_rows.shape, BF16),
            pltpu.VMEM((1, sat_count), jnp.int32),
            pltpu.VMEM((2, n_lat, row_count, half_count), BF16),
            pltpu.VMEM((n_lat, row_count, coef_width), BF16),
            pltpu.VMEM((slots, cap, width), BF16),
            pltpu.VMEM((n_src, cap, width), BF16),
            pltpu.VMEM((row_count, coef_width), BF16),
            pltpu.VMEM((half, width), F32),
            pltpu.VMEM((half, width), F32),
            pltpu.VMEM((total, half_count), BF16),
            pltpu.VMEM((2, total, half_count), BF16),
            dma((5,)), dma((half_count // half + 1,)),
            dma((n_lat,)), dma((n_lat,)), dma((n_lat,)), dma((n_lat,)),
            dma((n_src,)), dma((n_src,)), dma((2,)), dma((2,)),
        ],
        compiler_params=pltpu.CompilerParams(
            collective_id=0, has_side_effects=True, vmem_limit_bytes=60 * 2**20),
        name="exchange",
    )(
        order_value,
        deg_first,
        anomaly,
        row_weight,
        panel.reshape(group_orders, row_count, half_count),
        sat_rows,
        sat_slot.reshape(1, sat_count),
    )
    flat, right = pl.pallas_call(
        hand_out,
        out_shape=results,
        in_specs=[pl.BlockSpec(memory_space=pl.ANY)] * 2,
        out_specs=[hbm] * 2,
        scratch_shapes=[dma((2 * stripes + 1,))],
        name="hand_out",
    )(flat, right)
    normals = flat.reshape(half_count, stripes, 2, LANES).transpose(0, 2, 1, 3)
    normals = with_layout_constraint(normals, Layout((0, 2, 1, 3)))
    normals = normals.reshape(1, 1, 1, half_count, 2, half_count)
    return normals, right.reshape(1, 1, 2, 1, half_count)


def solution(mesh):
    sizes = (mesh.shape["lat"], mesh.shape["orb"])
    in_specs = (
        P(None, "lat", None),
        P(),
        P("orb", None, "lat", "ord", None),
        P("orb", None),
        P("orb", "lat"),
        P(("lat", "ord", "orb"), None),
        P(("lat", "ord", "orb"), None),
    )
    out_specs = (P("orb", "lat", "ord", None, None, None), P("orb", "lat", None, "ord", None))
    return jax.shard_map(
        functools.partial(shards, sizes), mesh=mesh, in_specs=in_specs,
        out_specs=out_specs, check_vma=False)
```

```python
import functools
import math

import jax
import jax.numpy as jnp
from jax import lax
from jax.experimental import pallas as pl
from jax.experimental.pallas import tpu as pltpu
from jax.experimental.layout import Layout, with_layout_constraint
from jax.sharding import PartitionSpec as P

LMAX = 2190
MESH = pl.DeviceIdType.MESH
F32 = jnp.float32
BF16 = jnp.bfloat16
LANES = 128


def iota(shape, dim):
    return lax.broadcasted_iota(jnp.int32, shape, dim)


def dot_tn(a, b):
    return lax.dot_general(a, b, (((0,), (0,)), ((), ())), preferred_element_type=F32)


def dot_nt(a, b):
    return lax.dot_general(a, b, (((1,), (1,)), ((), ())), preferred_element_type=F32)


def dot_nn(a, b):
    return jnp.dot(a, b, preferred_element_type=F32)


def exchange_kernel(
    sizes,
    order, first, anomaly_hbm, weight_hbm, panel, sat_hbm, slot_hbm,
    out_hbm, right_hbm,
    out, right, anomaly, weight, sat_rows, slot_row, panels, coefs,
    bucket, arrived, coef_mine, gram_send, gram_recv, left, sides,
    load, save, panel_s, panel_r, coef_s, coef_r, sat_s, sat_r, pair_s, pair_r,
):
    n_lat, n_orb = sizes
    group_orders, row_count, half_count = panel.shape
    sat_count, width = sat_rows.shape
    half = width // 2
    cap = bucket.shape[1]
    slots = bucket.shape[0]
    n_src = n_lat * n_orb
    lon = anomaly.shape[2]
    lat = lax.axis_index("lat")
    par = lax.axis_index("ord")
    orb = lax.axis_index("orb")
    other = 1 - par
    stripes = half_count // LANES
    base = first[0, 0]
    limit = LMAX - base
    me = lat * n_orb + orb

    def peer(k):
        p = lax.rem(me + k, n_src)
        return p, p // n_orb, lax.rem(p, n_orb)

    loads = [
        pltpu.make_async_copy(sat_hbm, sat_rows, load.at[0]),
        pltpu.make_async_copy(slot_hbm, slot_row, load.at[1]),
        pltpu.make_async_copy(anomaly_hbm, anomaly, load.at[2]),
        pltpu.make_async_copy(weight_hbm, weight, load.at[3]),
        pltpu.make_async_copy(panel.at[lat], panels.at[par, lat], load.at[4]),
    ]
    for one in loads:
        one.start()
    barrier = pltpu.get_barrier_semaphore()
    pl.semaphore_signal(barrier, inc=1, device_id=(lat, other, orb), device_id_type=MESH)

    def greet(k, c):
        _, a, b = peer(k)
        pl.semaphore_signal(barrier, inc=1, device_id=(a, par, b), device_id_type=MESH)
        return c

    lax.fori_loop(1, n_src, greet, 0)

    def panel_copy(dst, src):
        return pltpu.make_async_remote_copy(
            src_ref=panel.at[dst], dst_ref=panels.at[par, src],
            send_sem=panel_s.at[dst], recv_sem=panel_r.at[src],
            device_id=(dst, par, orb), device_id_type=MESH)

    def sat_copy(dst, a, b, src):
        return pltpu.make_async_remote_copy(
            src_ref=bucket.at[b * group_orders + a], dst_ref=arrived.at[src],
            send_sem=sat_s.at[dst], recv_sem=sat_r.at[src],
            device_id=(a, par, b), device_id_type=MESH)

    def coef_copy(dst, src):
        return pltpu.make_async_remote_copy(
            src_ref=coef_mine, dst_ref=coefs.at[src],
            send_sem=coef_s.at[dst], recv_sem=coef_r.at[src],
            device_id=(dst, par, orb), device_id_type=MESH)

    def forward():
        return pltpu.make_async_remote_copy(
            src_ref=panels.at[par], dst_ref=panels.at[par],
            send_sem=pair_s.at[0], recv_sem=pair_r.at[0],
            device_id=(lat, other, orb), device_id_type=MESH)

    def backward():
        return pltpu.make_async_remote_copy(
            src_ref=panels.at[par], dst_ref=panels.at[other],
            send_sem=pair_s.at[0], recv_sem=pair_r.at[0],
            device_id=(lat, other, orb), device_id_type=MESH)

    def gram_copy():
        return pltpu.make_async_remote_copy(
            src_ref=gram_send, dst_ref=gram_recv,
            send_sem=pair_s.at[1], recv_sem=pair_r.at[1],
            device_id=(lat, other, orb), device_id_type=MESH)

    def each_lat(action):
        def body(k, c):
            action(lax.rem(lat + k, n_lat))
            return c

        lax.fori_loop(1, n_lat, body, 0)

    def each_src(action):
        def body(k, c):
            action(*peer(k))
            return c

        lax.fori_loop(1, n_src, body, 0)

    loads[0].wait()
    loads[1].wait()
    perm = (iota((width, width), 0)
            == 2 * (iota((width, width), 1) % half) + iota((width, width), 1) // half)
    split_rows = dot_nn(sat_rows[...], perm.astype(F32).astype(BF16)).astype(BF16)
    row = slot_row[...].astype(F32)
    sub = iota((sat_count, sat_count), 0)
    lane = iota((sat_count, sat_count), 1)
    column = jnp.sum(jnp.where(sub == lane, row, 0.0), axis=1, keepdims=True)
    earlier = (column == row) & (sub < lane)
    rank = jnp.sum(jnp.where(earlier, 1.0, 0.0), axis=0, keepdims=True)
    target = row * float(cap) + rank
    pl.semaphore_wait(barrier, n_src)
    each_lat(lambda dst: panel_copy(dst, lat).start())
    step_slots = max(1, min(slots, 512 // cap))

    def fill(i, c):
        spot = (iota((step_slots * cap, sat_count), 0) + i * (step_slots * cap)).astype(F32)
        hot = jnp.where(spot == target, 1.0, 0.0).astype(BF16)
        rows = dot_nn(hot, split_rows).astype(BF16)
        bucket[pl.ds(i * step_slots, step_slots)] = rows.reshape(step_slots, cap, width)
        return c

    if slots == step_slots:
        fill(0, 0)
    else:
        lax.fori_loop(0, slots // step_slots, fill, 0)

    each_src(lambda p, a, b: sat_copy(p, a, b, me).start())
    arrived[me] = bucket[orb * group_orders + lat]
    loads[2].wait()
    loads[3].wait()
    loads[4].wait()

    wide = 2 * group_orders
    line = iota((wide, 1), 0)
    order_col = jnp.zeros((wide, 1), F32)
    for o in range(group_orders):
        order_col = jnp.where(
            lax.rem(line, group_orders) == o, order[0, o].astype(F32), order_col)
    sample = iota((wide, lon), 1).astype(F32)
    x = sample * order_col
    r = x - jnp.floor(x * (1.0 / lon)) * float(lon)
    r = r - jnp.where(iota((wide, lon), 0) >= group_orders, lon / 4.0, 0.0)
    r = r - jnp.floor(r * (1.0 / lon) + 0.5) * float(lon)
    z = (lon / 4.0 - jnp.abs(r)) * (2.0 * math.pi / lon)
    z2 = z * z
    poly = -1.0 / math.factorial(11)
    for d in (9, 7, 5, 3, 1):
        sgn = 1.0 if d % 4 == 1 else -1.0
        poly = poly * z2 + sgn / math.factorial(d)
    trig = poly * z
    high = trig.astype(BF16)
    low = (trig - high.astype(F32)).astype(BF16)
    coef_mine[...] = jnp.zeros_like(coef_mine)
    total_rows = weight.shape[1]
    here = (iota((row_count, total_rows), 1)
            == iota((row_count, total_rows), 0) + lat * row_count)
    scale = math.sqrt(2.0 / lon)
    for h in range(2):
        data = anomaly[h]
        spectrum = (dot_nt(data, high) + dot_nt(data, low)) * scale
        own_weight = jnp.sum(
            jnp.where(here, weight[h:h + 1, :], 0.0), axis=1, keepdims=True)
        coef_mine[:, h * wide:(h + 1) * wide] = (spectrum * own_weight).astype(BF16)
    each_lat(lambda dst: coef_copy(dst, lat).start())
    coefs[lat] = coef_mine[...]

    each_lat(lambda src: panel_copy(src, src).wait_recv())
    forward().start()
    for l in range(n_lat):
        rows = slice(l * row_count, (l + 1) * row_count)
        live = 2 * iota((row_count, half_count), 1) + par <= limit
        left[rows, :] = jnp.where(live, panels[par, l].astype(F32), 0.0).astype(BF16)
    each_lat(lambda src: coef_copy(src, src).wait_recv())
    sign = 1.0 - 2.0 * lax.rem(base + par + order[0, lat], 2).astype(F32)
    products = dot_tn(coefs[...].reshape(total_rows, coefs.shape[2]), left[...])
    place = iota(products.shape, 0)
    for t in range(2):
        spot = t * group_orders + lat
        factor = jnp.where(place == spot, 1.0, jnp.where(place == wide + spot, sign, 0.0))
        right[t] = jnp.sum(products * factor, axis=0, keepdims=True)
    backward().wait_recv()
    for l in range(n_lat):
        rows = slice(l * row_count, (l + 1) * row_count)
        here = (iota((row_count, total_rows), 1)
                == iota((row_count, total_rows), 0) + l * row_count)
        north = jnp.sum(jnp.where(here, weight[0:1, :], 0.0), axis=1, keepdims=True)
        south = jnp.sum(jnp.where(here, weight[1:2, :], 0.0), axis=1, keepdims=True)
        for q in range(2):
            live = 2 * iota((row_count, half_count), 1) + q <= limit
            masked = jnp.where(live, panels[q, l].astype(F32), 0.0)
            factor = jnp.where(par == q, north + south, north - south)
            sides[q, rows, :] = (masked * factor).astype(BF16)

    def grid_tile(i):
        block = left[:, i * half:(i + 1) * half]
        for q in range(2):
            value = dot_tn(block, sides[q])
            for b in range(stripes):
                at = pl.ds(i * half * 2 * stripes + 2 * b + q, half, stride=2 * stripes)
                out[at, :] = value[:, b * LANES:(b + 1) * LANES]

    def save_tile(i):
        span = pl.ds(i * half * 2 * stripes, half * 2 * stripes)
        return pltpu.make_async_copy(out.at[span], out_hbm.at[span], save.at[i])

    tiles = half_count // half
    save_right = pltpu.make_async_copy(right, right_hbm, save.at[tiles])
    save_right.start()
    for i in range(1, tiles):
        grid_tile(i)
        save_tile(i).start()
    each_src(lambda p, a, b: sat_copy(p, a, b, p).wait_recv())

    chunk = max(1, min(n_src, 512 // cap))
    steps = n_src // chunk

    def gram(which):
        cols = pl.ds(pl.multiple_of(which * half, half), half)

        def part(i):
            full = arrived[pl.ds(i * chunk, chunk)].reshape(chunk * cap, width)
            some = arrived[pl.ds(i * chunk, chunk), :, cols].reshape(chunk * cap, half)
            return dot_tn(some, full)

        if steps == 1:
            return part(0)
        return lax.fori_loop(
            0, steps, lambda i, c: c + part(i), jnp.zeros((half, width), F32))

    gram_send[...] = gram(other)
    gram_copy().start()
    own = gram(par)
    grid_tile(0)
    gram_copy().wait_recv()
    summed = own + gram_recv[...]
    for q in range(2):
        for b in range(half // LANES):
            at = pl.ds(2 * b + q, half, stride=2 * stripes)
            keep = ((2 * iota((half, LANES), 0) + par <= limit)
                    & (2 * (iota((half, LANES), 1) + b * LANES) + q <= limit))
            piece = summed[:, q * half + b * LANES:q * half + (b + 1) * LANES]
            out[at, :] = out[at, :] + jnp.where(keep, piece, 0.0)
    save_tile(0).start()
    each_lat(lambda dst: panel_copy(dst, lat).wait_send())
    each_lat(lambda dst: coef_copy(dst, lat).wait_send())
    each_src(lambda p, a, b: sat_copy(p, a, b, me).wait_send())
    forward().wait_send()
    gram_copy().wait_send()
    save_right.wait()
    for i in range(tiles):
        save_tile(i).wait()


def hand_out(flat, side, out, right, held, held_side, sem_in, sem_out):
    parts = sem_in.shape[0] - 1
    rows = flat.shape[0] // parts

    def pair(i):
        if i == parts:
            return (pltpu.make_async_copy(side, held_side, sem_in.at[i]),
                    pltpu.make_async_copy(held_side, right, sem_out.at[i]))
        span = pl.ds(i * rows, rows)
        return (pltpu.make_async_copy(flat.at[span], held.at[span], sem_in.at[i]),
                pltpu.make_async_copy(held.at[span], out.at[span], sem_out.at[i]))

    pairs = [pair(i) for i in range(parts + 1)]
    for fetch, _ in pairs:
        fetch.start()
    for fetch, store in pairs:
        fetch.wait()
        store.start()
    for _, store in pairs:
        store.wait()


def shards(sizes, anomaly, row_weight, panel, order_value, deg_first, sat_rows, sat_slot):
    n_lat, n_orb = sizes
    _, group_orders, row_count, _, half_count = panel.shape
    sat_count, width = sat_rows.shape
    half = width // 2
    total = n_lat * row_count
    slots = n_orb * group_orders
    n_src = n_lat * n_orb
    cap = max(16, 2 * sat_count // slots)
    smem = pl.BlockSpec(memory_space=pltpu.SMEM)
    dma = pltpu.SemaphoreType.DMA
    hbm = pl.BlockSpec(memory_space=pltpu.HBM)
    stripes = half_count // LANES
    coef_width = -(-4 * group_orders // LANES) * LANES
    results = (
        jax.ShapeDtypeStruct((half_count * 2 * stripes, LANES), F32),
        jax.ShapeDtypeStruct((2, 1, half_count), F32),
    )
    flat, right = pl.pallas_call(
        functools.partial(exchange_kernel, sizes),
        out_shape=results,
        in_specs=[smem] * 2 + [hbm] * 5,
        out_specs=[hbm] * 2,
        scratch_shapes=[
            pltpu.VMEM(results[0].shape, F32),
            pltpu.VMEM(results[1].shape, F32),
            pltpu.VMEM(anomaly.shape, BF16),
            pltpu.VMEM(row_weight.shape, F32),
            pltpu.VMEM(sat_rows.shape, BF16),
            pltpu.VMEM((1, sat_count), jnp.int32),
            pltpu.VMEM((2, n_lat, row_count, half_count), BF16),
            pltpu.VMEM((n_lat, row_count, coef_width), BF16),
            pltpu.VMEM((slots, cap, width), BF16),
            pltpu.VMEM((n_src, cap, width), BF16),
            pltpu.VMEM((row_count, coef_width), BF16),
            pltpu.VMEM((half, width), F32),
            pltpu.VMEM((half, width), F32),
            pltpu.VMEM((total, half_count), BF16),
            pltpu.VMEM((2, total, half_count), BF16),
            dma((5,)), dma((half_count // half + 1,)),
            dma((n_lat,)), dma((n_lat,)), dma((n_lat,)), dma((n_lat,)),
            dma((n_src,)), dma((n_src,)), dma((2,)), dma((2,)),
        ],
        compiler_params=pltpu.CompilerParams(
            collective_id=0, has_side_effects=True, vmem_limit_bytes=60 * 2**20),
        name="exchange",
    )(
        order_value,
        deg_first,
        anomaly,
        row_weight,
        panel.reshape(group_orders, row_count, half_count),
        sat_rows,
        sat_slot.reshape(1, sat_count),
    )
    flat, right = pl.pallas_call(
        hand_out,
        out_shape=results,
        in_specs=[pl.BlockSpec(memory_space=pl.ANY)] * 2,
        out_specs=[hbm] * 2,
        scratch_shapes=[
            pltpu.VMEM(results[0].shape, F32),
            pltpu.VMEM(results[1].shape, F32),
            dma((2 * stripes + 1,)),
            dma((2 * stripes + 1,)),
        ],
        compiler_params=pltpu.CompilerParams(vmem_limit_bytes=60 * 2**20),
        name="hand_out",
    )(flat, right)
    normals = flat.reshape(half_count, stripes, 2, LANES).transpose(0, 2, 1, 3)
    normals = with_layout_constraint(normals, Layout((0, 2, 1, 3)))
    normals = normals.reshape(1, 1, 1, half_count, 2, half_count)
    return normals, right.reshape(1, 1, 2, 1, half_count)


def solution(mesh):
    sizes = (mesh.shape["lat"], mesh.shape["orb"])
    in_specs = (
        P(None, "lat", None),
        P(),
        P("orb", None, "lat", "ord", None),
        P("orb", None),
        P("orb", "lat"),
        P(("lat", "ord", "orb"), None),
        P(("lat", "ord", "orb"), None),
    )
    out_specs = (P("orb", "lat", "ord", None, None, None), P("orb", "lat", None, "ord", None))
    return jax.shard_map(
        functools.partial(shards, sizes), mesh=mesh, in_specs=in_specs,
        out_specs=out_specs, check_vma=False)
```

```python
import functools
import math

import jax
import jax.numpy as jnp
from jax import lax
from jax.experimental import pallas as pl
from jax.experimental.pallas import tpu as pltpu
from jax.experimental.layout import Layout, with_layout_constraint
from jax.sharding import PartitionSpec as P

LMAX = 2190
MESH = pl.DeviceIdType.MESH
F32 = jnp.float32
BF16 = jnp.bfloat16
LANES = 128


def iota(shape, dim):
    return lax.broadcasted_iota(jnp.int32, shape, dim)


def dot_tn(a, b):
    return lax.dot_general(a, b, (((0,), (0,)), ((), ())), preferred_element_type=F32)


def dot_nt(a, b):
    return lax.dot_general(a, b, (((1,), (1,)), ((), ())), preferred_element_type=F32)


def dot_nn(a, b):
    return jnp.dot(a, b, preferred_element_type=F32)


def exchange_kernel(
    sizes,
    order, first, anomaly_hbm, weight_hbm, panel, sat_hbm, slot_hbm,
    left_hbm, sides_hbm, sat_out, right_hbm,
    right, anomaly, weight, sat_rows, slot_row, panels, coefs,
    bucket, arrived, coef_mine, gram_send, gram_recv, left, sides,
    load, save, panel_s, panel_r, coef_s, coef_r, sat_s, sat_r, pair_s, pair_r,
):
    n_lat, n_orb = sizes
    group_orders, row_count, half_count = panel.shape
    sat_count, width = sat_rows.shape
    half = width // 2
    cap = bucket.shape[1]
    slots = bucket.shape[0]
    n_src = n_lat * n_orb
    lon = anomaly.shape[2]
    lat = lax.axis_index("lat")
    par = lax.axis_index("ord")
    orb = lax.axis_index("orb")
    other = 1 - par
    base = first[0, 0]
    limit = LMAX - base
    me = lat * n_orb + orb

    def peer(k):
        p = lax.rem(me + k, n_src)
        return p, p // n_orb, lax.rem(p, n_orb)

    loads = [
        pltpu.make_async_copy(sat_hbm, sat_rows, load.at[0]),
        pltpu.make_async_copy(slot_hbm, slot_row, load.at[1]),
        pltpu.make_async_copy(anomaly_hbm, anomaly, load.at[2]),
        pltpu.make_async_copy(weight_hbm, weight, load.at[3]),
        pltpu.make_async_copy(panel.at[lat], panels.at[par, lat], load.at[4]),
    ]
    for one in loads:
        one.start()
    barrier = pltpu.get_barrier_semaphore()
    pl.semaphore_signal(barrier, inc=1, device_id=(lat, other, orb), device_id_type=MESH)

    def greet(k, c):
        _, a, b = peer(k)
        pl.semaphore_signal(barrier, inc=1, device_id=(a, par, b), device_id_type=MESH)
        return c

    lax.fori_loop(1, n_src, greet, 0)

    def panel_copy(dst, src):
        return pltpu.make_async_remote_copy(
            src_ref=panel.at[dst], dst_ref=panels.at[par, src],
            send_sem=panel_s.at[dst], recv_sem=panel_r.at[src],
            device_id=(dst, par, orb), device_id_type=MESH)

    def sat_copy(dst, a, b, src):
        return pltpu.make_async_remote_copy(
            src_ref=bucket.at[b * group_orders + a], dst_ref=arrived.at[src],
            send_sem=sat_s.at[dst], recv_sem=sat_r.at[src],
            device_id=(a, par, b), device_id_type=MESH)

    def coef_copy(dst, src):
        return pltpu.make_async_remote_copy(
            src_ref=coef_mine, dst_ref=coefs.at[src],
            send_sem=coef_s.at[dst], recv_sem=coef_r.at[src],
            device_id=(dst, par, orb), device_id_type=MESH)

    def forward():
        return pltpu.make_async_remote_copy(
            src_ref=panels.at[par], dst_ref=panels.at[par],
            send_sem=pair_s.at[0], recv_sem=pair_r.at[0],
            device_id=(lat, other, orb), device_id_type=MESH)

    def backward():
        return pltpu.make_async_remote_copy(
            src_ref=panels.at[par], dst_ref=panels.at[other],
            send_sem=pair_s.at[0], recv_sem=pair_r.at[0],
            device_id=(lat, other, orb), device_id_type=MESH)

    def gram_copy():
        return pltpu.make_async_remote_copy(
            src_ref=gram_send, dst_ref=gram_recv,
            send_sem=pair_s.at[1], recv_sem=pair_r.at[1],
            device_id=(lat, other, orb), device_id_type=MESH)

    def each_lat(action):
        def body(k, c):
            action(lax.rem(lat + k, n_lat))
            return c

        lax.fori_loop(1, n_lat, body, 0)

    def each_src(action):
        def body(k, c):
            action(*peer(k))
            return c

        lax.fori_loop(1, n_src, body, 0)

    loads[0].wait()
    loads[1].wait()
    perm = (iota((width, width), 0)
            == 2 * (iota((width, width), 1) % half) + iota((width, width), 1) // half)
    split_rows = dot_nn(sat_rows[...], perm.astype(F32).astype(BF16)).astype(BF16)
    row = slot_row[...].astype(F32)
    sub = iota((sat_count, sat_count), 0)
    lane = iota((sat_count, sat_count), 1)
    column = jnp.sum(jnp.where(sub == lane, row, 0.0), axis=1, keepdims=True)
    earlier = (column == row) & (sub < lane)
    rank = jnp.sum(jnp.where(earlier, 1.0, 0.0), axis=0, keepdims=True)
    target = row * float(cap) + rank
    pl.semaphore_wait(barrier, n_src)
    each_lat(lambda dst: panel_copy(dst, lat).start())
    step_slots = max(1, min(slots, 512 // cap))

    def fill(i, c):
        spot = (iota((step_slots * cap, sat_count), 0) + i * (step_slots * cap)).astype(F32)
        hot = jnp.where(spot == target, 1.0, 0.0).astype(BF16)
        rows = dot_nn(hot, split_rows).astype(BF16)
        bucket[pl.ds(i * step_slots, step_slots)] = rows.reshape(step_slots, cap, width)
        return c

    if slots == step_slots:
        fill(0, 0)
    else:
        lax.fori_loop(0, slots // step_slots, fill, 0)

    each_src(lambda p, a, b: sat_copy(p, a, b, me).start())
    arrived[me] = bucket[orb * group_orders + lat]
    loads[2].wait()
    loads[3].wait()
    loads[4].wait()

    wide = 2 * group_orders
    line = iota((wide, 1), 0)
    order_col = jnp.zeros((wide, 1), F32)
    for o in range(group_orders):
        order_col = jnp.where(
            lax.rem(line, group_orders) == o, order[0, o].astype(F32), order_col)
    sample = iota((wide, lon), 1).astype(F32)
    x = sample * order_col
    r = x - jnp.floor(x * (1.0 / lon)) * float(lon)
    r = r - jnp.where(iota((wide, lon), 0) >= group_orders, lon / 4.0, 0.0)
    r = r - jnp.floor(r * (1.0 / lon) + 0.5) * float(lon)
    z = (lon / 4.0 - jnp.abs(r)) * (2.0 * math.pi / lon)
    z2 = z * z
    poly = -1.0 / math.factorial(11)
    for d in (9, 7, 5, 3, 1):
        sgn = 1.0 if d % 4 == 1 else -1.0
        poly = poly * z2 + sgn / math.factorial(d)
    trig = poly * z
    high = trig.astype(BF16)
    low = (trig - high.astype(F32)).astype(BF16)
    coef_mine[...] = jnp.zeros_like(coef_mine)
    total_rows = weight.shape[1]
    here = (iota((row_count, total_rows), 1)
            == iota((row_count, total_rows), 0) + lat * row_count)
    scale = math.sqrt(2.0 / lon)
    for h in range(2):
        data = anomaly[h]
        spectrum = (dot_nt(data, high) + dot_nt(data, low)) * scale
        own_weight = jnp.sum(
            jnp.where(here, weight[h:h + 1, :], 0.0), axis=1, keepdims=True)
        coef_mine[:, h * wide:(h + 1) * wide] = (spectrum * own_weight).astype(BF16)
    each_lat(lambda dst: coef_copy(dst, lat).start())
    coefs[lat] = coef_mine[...]

    each_lat(lambda src: panel_copy(src, src).wait_recv())
    forward().start()
    for l in range(n_lat):
        rows = slice(l * row_count, (l + 1) * row_count)
        live = 2 * iota((row_count, half_count), 1) + par <= limit
        left[rows, :] = jnp.where(live, panels[par, l].astype(F32), 0.0).astype(BF16)
    saves = [
        pltpu.make_async_copy(right, right_hbm, save.at[0]),
        pltpu.make_async_copy(left, left_hbm, save.at[1]),
        pltpu.make_async_copy(sides, sides_hbm, save.at[2]),
        pltpu.make_async_copy(gram_recv, sat_out, save.at[3]),
    ]
    saves[1].start()
    each_lat(lambda src: coef_copy(src, src).wait_recv())
    sign = 1.0 - 2.0 * lax.rem(base + par + order[0, lat], 2).astype(F32)
    products = dot_tn(coefs[...].reshape(total_rows, coefs.shape[2]), left[...])
    place = iota(products.shape, 0)
    for t in range(2):
        spot = t * group_orders + lat
        factor = jnp.where(place == spot, 1.0, jnp.where(place == wide + spot, sign, 0.0))
        right[t] = jnp.sum(products * factor, axis=0, keepdims=True)
    saves[0].start()
    backward().wait_recv()
    for l in range(n_lat):
        rows = slice(l * row_count, (l + 1) * row_count)
        here = (iota((row_count, total_rows), 1)
                == iota((row_count, total_rows), 0) + l * row_count)
        north = jnp.sum(jnp.where(here, weight[0:1, :], 0.0), axis=1, keepdims=True)
        south = jnp.sum(jnp.where(here, weight[1:2, :], 0.0), axis=1, keepdims=True)
        for q in range(2):
            live = 2 * iota((row_count, half_count), 1) + q <= limit
            masked = jnp.where(live, panels[q, l].astype(F32), 0.0)
            factor = jnp.where(par == q, north + south, north - south)
            sides[q, rows, :] = (masked * factor).astype(BF16)

    saves[2].start()
    each_src(lambda p, a, b: sat_copy(p, a, b, p).wait_recv())

    chunk = max(1, min(n_src, 512 // cap))
    steps = n_src // chunk

    def gram(which):
        cols = pl.ds(pl.multiple_of(which * half, half), half)

        def part(i):
            full = arrived[pl.ds(i * chunk, chunk)].reshape(chunk * cap, width)
            some = arrived[pl.ds(i * chunk, chunk), :, cols].reshape(chunk * cap, half)
            return dot_tn(some, full)

        if steps == 1:
            return part(0)
        return lax.fori_loop(
            0, steps, lambda i, c: c + part(i), jnp.zeros((half, width), F32))

    gram_send[...] = gram(other)
    gram_copy().start()
    own = gram(par)
    gram_copy().wait_recv()
    spot = iota((half, width), 1)
    keep = ((2 * iota((half, width), 0) + par <= limit)
            & (2 * lax.rem(spot, half) + spot // half <= limit))
    gram_recv[...] = jnp.where(keep, own + gram_recv[...], 0.0)
    saves[3].start()
    each_lat(lambda dst: panel_copy(dst, lat).wait_send())
    each_lat(lambda dst: coef_copy(dst, lat).wait_send())
    each_src(lambda p, a, b: sat_copy(p, a, b, me).wait_send())
    forward().wait_send()
    gram_copy().wait_send()
    for one in saves:
        one.wait()


def normal_kernel(
    left_hbm, sides_hbm, sat_hbm, right_hbm, out, right_out,
    left, sides, sat, right, flat, sem_in, sem_out,
):
    fetches = [
        pltpu.make_async_copy(left_hbm, left, sem_in.at[0]),
        pltpu.make_async_copy(sides_hbm, sides, sem_in.at[1]),
        pltpu.make_async_copy(sat_hbm, sat, sem_in.at[2]),
        pltpu.make_async_copy(right_hbm, right, sem_in.at[3]),
    ]
    for one in fetches:
        one.start()
    half, width = sat.shape
    half_count = left.shape[1]
    tiles = half_count // half
    stripes = half_count // LANES
    rows = half * 2 * stripes
    fetches[0].wait()
    fetches[1].wait()
    stores = []
    for i in list(range(1, tiles)) + [0]:
        if i == 0:
            fetches[2].wait()
        block = left[:, i * half:(i + 1) * half]
        for q in range(2):
            value = dot_tn(block, sides[q])
            for b in range(stripes):
                piece = value[:, b * LANES:(b + 1) * LANES]
                if i == 0 and b < half // LANES:
                    at = q * half + b * LANES
                    piece = piece + sat[:, at:at + LANES]
                flat[pl.ds(i * rows + 2 * b + q, half, stride=2 * stripes), :] = piece
        span = pl.ds(i * rows, rows)
        stores.append(pltpu.make_async_copy(flat.at[span], out.at[span], sem_out.at[i]))
        stores[-1].start()
    fetches[3].wait()
    stores.append(pltpu.make_async_copy(right, right_out, sem_out.at[tiles]))
    stores[-1].start()
    for one in stores:
        one.wait()


def shards(sizes, anomaly, row_weight, panel, order_value, deg_first, sat_rows, sat_slot):
    n_lat, n_orb = sizes
    _, group_orders, row_count, _, half_count = panel.shape
    sat_count, width = sat_rows.shape
    half = width // 2
    total = n_lat * row_count
    slots = n_orb * group_orders
    n_src = n_lat * n_orb
    cap = max(16, 2 * sat_count // slots)
    smem = pl.BlockSpec(memory_space=pltpu.SMEM)
    dma = pltpu.SemaphoreType.DMA
    hbm = pl.BlockSpec(memory_space=pltpu.HBM)
    stripes = half_count // LANES
    coef_width = -(-4 * group_orders // LANES) * LANES
    tiles = half_count // half
    left_type = jax.ShapeDtypeStruct((total, half_count), BF16)
    sides_type = jax.ShapeDtypeStruct((2, total, half_count), BF16)
    sat_type = jax.ShapeDtypeStruct((half, width), F32)
    right_type = jax.ShapeDtypeStruct((2, 1, half_count), F32)
    flat_type = jax.ShapeDtypeStruct((half_count * 2 * stripes, LANES), F32)
    left, sides, sat, right = pl.pallas_call(
        functools.partial(exchange_kernel, sizes),
        out_shape=(left_type, sides_type, sat_type, right_type),
        in_specs=[smem] * 2 + [hbm] * 5,
        out_specs=[hbm] * 4,
        scratch_shapes=[
            pltpu.VMEM(right_type.shape, F32),
            pltpu.VMEM(anomaly.shape, BF16),
            pltpu.VMEM(row_weight.shape, F32),
            pltpu.VMEM(sat_rows.shape, BF16),
            pltpu.VMEM((1, sat_count), jnp.int32),
            pltpu.VMEM((2, n_lat, row_count, half_count), BF16),
            pltpu.VMEM((n_lat, row_count, coef_width), BF16),
            pltpu.VMEM((slots, cap, width), BF16),
            pltpu.VMEM((n_src, cap, width), BF16),
            pltpu.VMEM((row_count, coef_width), BF16),
            pltpu.VMEM((half, width), F32),
            pltpu.VMEM((half, width), F32),
            pltpu.VMEM((total, half_count), BF16),
            pltpu.VMEM((2, total, half_count), BF16),
            dma((5,)), dma((4,)),
            dma((n_lat,)), dma((n_lat,)), dma((n_lat,)), dma((n_lat,)),
            dma((n_src,)), dma((n_src,)), dma((2,)), dma((2,)),
        ],
        compiler_params=pltpu.CompilerParams(
            collective_id=0, has_side_effects=True, vmem_limit_bytes=60 * 2**20),
        name="exchange",
    )(
        order_value,
        deg_first,
        anomaly,
        row_weight,
        panel.reshape(group_orders, row_count, half_count),
        sat_rows,
        sat_slot.reshape(1, sat_count),
    )
    flat, right = pl.pallas_call(
        normal_kernel,
        out_shape=(flat_type, right_type),
        in_specs=[pl.BlockSpec(memory_space=pl.ANY)] * 4,
        out_specs=[hbm] * 2,
        scratch_shapes=[
            pltpu.VMEM(t.shape, t.dtype)
            for t in (left_type, sides_type, sat_type, right_type, flat_type)
        ] + [dma((4,)), dma((tiles + 1,))],
        compiler_params=pltpu.CompilerParams(vmem_limit_bytes=60 * 2**20),
        name="normal",
    )(left, sides, sat, right)
    normals = flat.reshape(half_count, stripes, 2, LANES).transpose(0, 2, 1, 3)
    normals = with_layout_constraint(normals, Layout((0, 2, 1, 3)))
    normals = normals.reshape(1, 1, 1, half_count, 2, half_count)
    return normals, right.reshape(1, 1, 2, 1, half_count)


def solution(mesh):
    sizes = (mesh.shape["lat"], mesh.shape["orb"])
    in_specs = (
        P(None, "lat", None),
        P(),
        P("orb", None, "lat", "ord", None),
        P("orb", None),
        P("orb", "lat"),
        P(("lat", "ord", "orb"), None),
        P(("lat", "ord", "orb"), None),
    )
    out_specs = (P("orb", "lat", "ord", None, None, None), P("orb", "lat", None, "ord", None))
    return jax.shard_map(
        functools.partial(shards, sizes), mesh=mesh, in_specs=in_specs,
        out_specs=out_specs, check_vma=False)
```

```python
import functools
import math

import jax
import jax.numpy as jnp
from jax import lax
from jax.experimental import pallas as pl
from jax.experimental.pallas import tpu as pltpu
from jax.experimental.layout import Layout, with_layout_constraint
from jax.sharding import PartitionSpec as P

LMAX = 2190
MESH = pl.DeviceIdType.MESH
F32 = jnp.float32
BF16 = jnp.bfloat16
LANES = 128


def iota(shape, dim):
    return lax.broadcasted_iota(jnp.int32, shape, dim)


def dot_tn(a, b):
    return lax.dot_general(a, b, (((0,), (0,)), ((), ())), preferred_element_type=F32)


def dot_nt(a, b):
    return lax.dot_general(a, b, (((1,), (1,)), ((), ())), preferred_element_type=F32)


def dot_nn(a, b):
    return jnp.dot(a, b, preferred_element_type=F32)


def exchange_kernel(
    sizes,
    order, first, anomaly_hbm, weight_hbm, panel, sat_hbm, slot_hbm,
    left_hbm, sides_hbm, sat_out, right_hbm,
    right, anomaly, weight, sat_rows, slot_row, panels, coefs,
    bucket, arrived, coef_mine, gram_send, gram_recv, left, sides,
    load, save, panel_s, panel_r, coef_s, coef_r, sat_s, sat_r, pair_s, pair_r,
):
    n_lat, n_orb = sizes
    group_orders, row_count, half_count = panel.shape
    sat_count, width = sat_rows.shape
    half = width // 2
    cap = bucket.shape[1]
    slots = bucket.shape[0]
    n_src = n_lat * n_orb
    lon = anomaly.shape[2]
    lat = lax.axis_index("lat")
    par = lax.axis_index("ord")
    orb = lax.axis_index("orb")
    other = 1 - par
    base = first[0, 0]
    limit = LMAX - base
    me = lat * n_orb + orb

    def peer(k):
        p = lax.rem(me + k, n_src)
        return p, p // n_orb, lax.rem(p, n_orb)

    loads = [
        pltpu.make_async_copy(sat_hbm, sat_rows, load.at[0]),
        pltpu.make_async_copy(slot_hbm, slot_row, load.at[1]),
        pltpu.make_async_copy(anomaly_hbm, anomaly, load.at[2]),
        pltpu.make_async_copy(weight_hbm, weight, load.at[3]),
        pltpu.make_async_copy(panel.at[lat], panels.at[par, lat], load.at[4]),
    ]
    for one in loads:
        one.start()
    barrier = pltpu.get_barrier_semaphore()
    pl.semaphore_signal(barrier, inc=1, device_id=(lat, other, orb), device_id_type=MESH)

    def greet(k, c):
        _, a, b = peer(k)
        pl.semaphore_signal(barrier, inc=1, device_id=(a, par, b), device_id_type=MESH)
        return c

    lax.fori_loop(1, n_src, greet, 0)

    def panel_copy(dst, src):
        return pltpu.make_async_remote_copy(
            src_ref=panel.at[dst], dst_ref=panels.at[par, src],
            send_sem=panel_s.at[dst], recv_sem=panel_r.at[src],
            device_id=(dst, par, orb), device_id_type=MESH)

    def sat_copy(dst, a, b, src):
        return pltpu.make_async_remote_copy(
            src_ref=bucket.at[b * group_orders + a], dst_ref=arrived.at[src],
            send_sem=sat_s.at[dst], recv_sem=sat_r.at[src],
            device_id=(a, par, b), device_id_type=MESH)

    def coef_copy(dst, src):
        return pltpu.make_async_remote_copy(
            src_ref=coef_mine, dst_ref=coefs.at[src],
            send_sem=coef_s.at[dst], recv_sem=coef_r.at[src],
            device_id=(dst, par, orb), device_id_type=MESH)

    def forward():
        return pltpu.make_async_remote_copy(
            src_ref=panels.at[par], dst_ref=panels.at[par],
            send_sem=pair_s.at[0], recv_sem=pair_r.at[0],
            device_id=(lat, other, orb), device_id_type=MESH)

    def backward():
        return pltpu.make_async_remote_copy(
            src_ref=panels.at[par], dst_ref=panels.at[other],
            send_sem=pair_s.at[0], recv_sem=pair_r.at[0],
            device_id=(lat, other, orb), device_id_type=MESH)

    def gram_copy():
        return pltpu.make_async_remote_copy(
            src_ref=gram_send, dst_ref=gram_recv,
            send_sem=pair_s.at[1], recv_sem=pair_r.at[1],
            device_id=(lat, other, orb), device_id_type=MESH)

    def each_lat(action):
        def body(k, c):
            action(lax.rem(lat + k, n_lat))
            return c

        lax.fori_loop(1, n_lat, body, 0)

    def each_src(action):
        def body(k, c):
            action(*peer(k))
            return c

        lax.fori_loop(1, n_src, body, 0)

    loads[0].wait()
    loads[1].wait()
    perm = (iota((width, width), 0)
            == 2 * (iota((width, width), 1) % half) + iota((width, width), 1) // half)
    split_rows = dot_nn(sat_rows[...], perm.astype(F32).astype(BF16)).astype(BF16)
    row = slot_row[...].astype(F32)
    sub = iota((sat_count, sat_count), 0)
    lane = iota((sat_count, sat_count), 1)
    column = jnp.sum(jnp.where(sub == lane, row, 0.0), axis=1, keepdims=True)
    earlier = (column == row) & (sub < lane)
    rank = jnp.sum(jnp.where(earlier, 1.0, 0.0), axis=0, keepdims=True)
    target = row * float(cap) + rank
    step_slots = max(1, min(slots, 512 // cap))

    def fill(i, c):
        spot = (iota((step_slots * cap, sat_count), 0) + i * (step_slots * cap)).astype(F32)
        hot = jnp.where(spot == target, 1.0, 0.0).astype(BF16)
        rows = dot_nn(hot, split_rows).astype(BF16)
        bucket[pl.ds(i * step_slots, step_slots)] = rows.reshape(step_slots, cap, width)
        return c

    if slots == step_slots:
        fill(0, 0)
    else:
        lax.fori_loop(0, slots // step_slots, fill, 0)

    pl.semaphore_wait(barrier, n_src)
    each_lat(lambda dst: panel_copy(dst, lat).start())
    each_src(lambda p, a, b: sat_copy(p, a, b, me).start())
    arrived[me] = bucket[orb * group_orders + lat]
    loads[2].wait()
    loads[3].wait()
    loads[4].wait()

    wide = 2 * group_orders
    line = iota((wide, 1), 0)
    order_col = jnp.zeros((wide, 1), F32)
    for o in range(group_orders):
        order_col = jnp.where(
            lax.rem(line, group_orders) == o, order[0, o].astype(F32), order_col)
    sample = iota((wide, lon), 1).astype(F32)
    x = sample * order_col
    r = x - jnp.floor(x * (1.0 / lon)) * float(lon)
    r = r - jnp.where(iota((wide, lon), 0) >= group_orders, lon / 4.0, 0.0)
    r = r - jnp.floor(r * (1.0 / lon) + 0.5) * float(lon)
    z = (lon / 4.0 - jnp.abs(r)) * (2.0 * math.pi / lon)
    z2 = z * z
    poly = -1.0 / math.factorial(11)
    for d in (9, 7, 5, 3, 1):
        sgn = 1.0 if d % 4 == 1 else -1.0
        poly = poly * z2 + sgn / math.factorial(d)
    trig = poly * z
    high = trig.astype(BF16)
    low = (trig - high.astype(F32)).astype(BF16)
    coef_mine[...] = jnp.zeros_like(coef_mine)
    total_rows = weight.shape[1]
    here = (iota((row_count, total_rows), 1)
            == iota((row_count, total_rows), 0) + lat * row_count)
    scale = math.sqrt(2.0 / lon)
    for h in range(2):
        data = anomaly[h]
        spectrum = (dot_nt(data, high) + dot_nt(data, low)) * scale
        own_weight = jnp.sum(
            jnp.where(here, weight[h:h + 1, :], 0.0), axis=1, keepdims=True)
        coef_mine[:, h * wide:(h + 1) * wide] = (spectrum * own_weight).astype(BF16)
    each_lat(lambda dst: coef_copy(dst, lat).start())
    coefs[lat] = coef_mine[...]

    each_lat(lambda src: panel_copy(src, src).wait_recv())
    forward().start()
    for l in range(n_lat):
        rows = slice(l * row_count, (l + 1) * row_count)
        live = 2 * iota((row_count, half_count), 1) + par <= limit
        left[rows, :] = jnp.where(live, panels[par, l].astype(F32), 0.0).astype(BF16)
    saves = [
        pltpu.make_async_copy(right, right_hbm, save.at[0]),
        pltpu.make_async_copy(left, left_hbm, save.at[1]),
        pltpu.make_async_copy(sides, sides_hbm, save.at[2]),
        pltpu.make_async_copy(gram_recv, sat_out, save.at[3]),
    ]
    saves[1].start()
    each_lat(lambda src: coef_copy(src, src).wait_recv())
    sign = 1.0 - 2.0 * lax.rem(base + par + order[0, lat], 2).astype(F32)
    products = dot_tn(coefs[...].reshape(total_rows, coefs.shape[2]), left[...])
    place = iota(products.shape, 0)
    for t in range(2):
        spot = t * group_orders + lat
        factor = jnp.where(place == spot, 1.0, jnp.where(place == wide + spot, sign, 0.0))
        right[t] = jnp.sum(products * factor, axis=0, keepdims=True)
    saves[0].start()
    backward().wait_recv()
    for l in range(n_lat):
        rows = slice(l * row_count, (l + 1) * row_count)
        here = (iota((row_count, total_rows), 1)
                == iota((row_count, total_rows), 0) + l * row_count)
        north = jnp.sum(jnp.where(here, weight[0:1, :], 0.0), axis=1, keepdims=True)
        south = jnp.sum(jnp.where(here, weight[1:2, :], 0.0), axis=1, keepdims=True)
        for q in range(2):
            live = 2 * iota((row_count, half_count), 1) + q <= limit
            masked = jnp.where(live, panels[q, l].astype(F32), 0.0)
            factor = jnp.where(par == q, north + south, north - south)
            sides[q, rows, :] = (masked * factor).astype(BF16)

    saves[2].start()
    each_src(lambda p, a, b: sat_copy(p, a, b, p).wait_recv())

    chunk = max(1, min(n_src, 512 // cap))
    steps = n_src // chunk

    def gram(which):
        cols = pl.ds(pl.multiple_of(which * half, half), half)

        def part(i):
            full = arrived[pl.ds(i * chunk, chunk)].reshape(chunk * cap, width)
            some = arrived[pl.ds(i * chunk, chunk), :, cols].reshape(chunk * cap, half)
            return dot_tn(some, full)

        if steps == 1:
            return part(0)
        return lax.fori_loop(
            0, steps, lambda i, c: c + part(i), jnp.zeros((half, width), F32))

    gram_send[...] = gram(other)
    gram_copy().start()
    own = gram(par)
    gram_copy().wait_recv()
    spot = iota((half, width), 1)
    keep = ((2 * iota((half, width), 0) + par <= limit)
            & (2 * lax.rem(spot, half) + spot // half <= limit))
    gram_recv[...] = jnp.where(keep, own + gram_recv[...], 0.0)
    saves[3].start()
    each_lat(lambda dst: panel_copy(dst, lat).wait_send())
    each_lat(lambda dst: coef_copy(dst, lat).wait_send())
    each_src(lambda p, a, b: sat_copy(p, a, b, me).wait_send())
    forward().wait_send()
    gram_copy().wait_send()
    for one in saves:
        one.wait()


def normal_kernel(
    left_hbm, sides_hbm, sat_hbm, right_hbm, out, right_out,
    left, sides, sat, right, flat, sem_in, sem_out,
):
    fetches = [
        pltpu.make_async_copy(left_hbm, left, sem_in.at[0]),
        pltpu.make_async_copy(sides_hbm, sides, sem_in.at[1]),
        pltpu.make_async_copy(sat_hbm, sat, sem_in.at[2]),
        pltpu.make_async_copy(right_hbm, right, sem_in.at[3]),
    ]
    for one in fetches:
        one.start()
    half, width = sat.shape
    half_count = left.shape[1]
    tiles = half_count // half
    stripes = half_count // LANES
    rows = half * 2 * stripes
    fetches[0].wait()
    fetches[1].wait()
    stores = []
    for i in list(range(1, tiles)) + [0]:
        if i == 0:
            fetches[2].wait()
        block = left[:, i * half:(i + 1) * half]
        for q in range(2):
            value = dot_tn(block, sides[q])
            for b in range(stripes):
                piece = value[:, b * LANES:(b + 1) * LANES]
                if i == 0 and b < half // LANES:
                    at = q * half + b * LANES
                    piece = piece + sat[:, at:at + LANES]
                flat[pl.ds(i * rows + 2 * b + q, half, stride=2 * stripes), :] = piece
        span = pl.ds(i * rows, rows)
        stores.append(pltpu.make_async_copy(flat.at[span], out.at[span], sem_out.at[i]))
        stores[-1].start()
    fetches[3].wait()
    stores.append(pltpu.make_async_copy(right, right_out, sem_out.at[tiles]))
    stores[-1].start()
    for one in stores:
        one.wait()


def shards(sizes, anomaly, row_weight, panel, order_value, deg_first, sat_rows, sat_slot):
    n_lat, n_orb = sizes
    _, group_orders, row_count, _, half_count = panel.shape
    sat_count, width = sat_rows.shape
    half = width // 2
    total = n_lat * row_count
    slots = n_orb * group_orders
    n_src = n_lat * n_orb
    cap = max(16, 2 * sat_count // slots)
    smem = pl.BlockSpec(memory_space=pltpu.SMEM)
    dma = pltpu.SemaphoreType.DMA
    hbm = pl.BlockSpec(memory_space=pltpu.HBM)
    stripes = half_count // LANES
    coef_width = -(-4 * group_orders // LANES) * LANES
    tiles = half_count // half
    left_type = jax.ShapeDtypeStruct((total, half_count), BF16)
    sides_type = jax.ShapeDtypeStruct((2, total, half_count), BF16)
    sat_type = jax.ShapeDtypeStruct((half, width), F32)
    right_type = jax.ShapeDtypeStruct((2, 1, half_count), F32)
    flat_type = jax.ShapeDtypeStruct((half_count * 2 * stripes, LANES), F32)
    left, sides, sat, right = pl.pallas_call(
        functools.partial(exchange_kernel, sizes),
        out_shape=(left_type, sides_type, sat_type, right_type),
        in_specs=[smem] * 2 + [hbm] * 5,
        out_specs=[hbm] * 4,
        scratch_shapes=[
            pltpu.VMEM(right_type.shape, F32),
            pltpu.VMEM(anomaly.shape, BF16),
            pltpu.VMEM(row_weight.shape, F32),
            pltpu.VMEM(sat_rows.shape, BF16),
            pltpu.VMEM((1, sat_count), jnp.int32),
            pltpu.VMEM((2, n_lat, row_count, half_count), BF16),
            pltpu.VMEM((n_lat, row_count, coef_width), BF16),
            pltpu.VMEM((slots, cap, width), BF16),
            pltpu.VMEM((n_src, cap, width), BF16),
            pltpu.VMEM((row_count, coef_width), BF16),
            pltpu.VMEM((half, width), F32),
            pltpu.VMEM((half, width), F32),
            pltpu.VMEM((total, half_count), BF16),
            pltpu.VMEM((2, total, half_count), BF16),
            dma((5,)), dma((4,)),
            dma((n_lat,)), dma((n_lat,)), dma((n_lat,)), dma((n_lat,)),
            dma((n_src,)), dma((n_src,)), dma((2,)), dma((2,)),
        ],
        compiler_params=pltpu.CompilerParams(
            collective_id=0, has_side_effects=True, vmem_limit_bytes=60 * 2**20),
        name="exchange",
    )(
        order_value,
        deg_first,
        anomaly,
        row_weight,
        panel.reshape(group_orders, row_count, half_count),
        sat_rows,
        sat_slot.reshape(1, sat_count),
    )
    flat, right = pl.pallas_call(
        normal_kernel,
        out_shape=(flat_type, right_type),
        in_specs=[pl.BlockSpec(memory_space=pl.ANY)] * 4,
        out_specs=[hbm] * 2,
        scratch_shapes=[
            pltpu.VMEM(t.shape, t.dtype)
            for t in (left_type, sides_type, sat_type, right_type, flat_type)
        ] + [dma((4,)), dma((tiles + 1,))],
        compiler_params=pltpu.CompilerParams(vmem_limit_bytes=60 * 2**20),
        name="normal",
    )(left, sides, sat, right)
    normals = flat.reshape(half_count, stripes, 2, LANES).transpose(0, 2, 1, 3)
    normals = with_layout_constraint(normals, Layout((0, 2, 1, 3)))
    normals = normals.reshape(1, 1, 1, half_count, 2, half_count)
    return normals, right.reshape(1, 1, 2, 1, half_count)


def solution(mesh):
    sizes = (mesh.shape["lat"], mesh.shape["orb"])
    in_specs = (
        P(None, "lat", None),
        P(),
        P("orb", None, "lat", "ord", None),
        P("orb", None),
        P("orb", "lat"),
        P(("lat", "ord", "orb"), None),
        P(("lat", "ord", "orb"), None),
    )
    out_specs = (P("orb", "lat", "ord", None, None, None), P("orb", "lat", None, "ord", None))
    return jax.shard_map(
        functools.partial(shards, sizes), mesh=mesh, in_specs=in_specs,
        out_specs=out_specs, check_vma=False)
```
